32 devices in a mesh: sib: 2 (over y), row: 4 (over z), col: 4 (over x, core).
Axes of the slice: x: 2, y: 2, z: 4, core: 2. Of those that a mesh axis runs over, the one named last changes fastest.
Arguments:
- eigvec: bfloat16 [2, 4096, 8192], P('sib', 'row', 'col'), may hold values from -6 to 6
- poles: float32 [2, 8192], P('sib', 'col'), may hold values from 0 to 8192, as said below
- weights: float32 [2, 8192], P('sib', 'col'), may hold values from -5 to 5
- shifts: float32 [2, 256], P('sib'), may hold values from 0 to 8192, as said below
- pair_src: int32 [2, 4, 512], P('sib', 'col'), may hold values from 0 to 2047, as said below
- pair_dst: int32 [2, 4, 512], P('sib', 'col'), may hold values from 0 to 2047, as said below
- rot_cos: float32 [2, 4, 512], P('sib', 'col'), may hold values from 0.3 to 1
- rot_sin: float32 [2, 4, 512], P('sib', 'col'), may hold values from -1 to 1
Outputs:
- merged: bfloat16 [8192, 256], P(('sib', 'row', 'col'))
The draws below stay inside these ranges and needn't reach their ends.
Inputs may be any that keep to these rules, and one draw needn't show every extreme that they name: Poles are dealt block-cyclically over col: poles[s, c * 2048 + i] equals i * 4 + c plus an offset in [0, 0.25], so every col index holds poles spaced 4 apart over the whole spectrum. shifts[s, j] equals j * 32 + (j % 4) + 0.5 plus an offset in [0, 0.25], so no shift comes within 0.25 of a pole. `pair_src`: for each sibling and col index the 512 entries are distinct local columns; 0 and 2047 are among them. `pair_dst`: for each sibling and col index the 512 entries are distinct local columns; 0 and 2047 are among them.
All inputs are finite; a program needn't handle non-finite values.
Results may differ from the reference program's by a relative error of at most 0.00175.
Values may be sent and summed in bfloat16 or wider, within the bound.
A program may use at most 64 MiB of HBM per device.

```python
import jax
import jax.numpy as jnp
import numpy as np
from jax import lax

K_DEV = 2048
SLAB = 256
R_DEV = 1024
PAIRS = 512
K = 8192
ROWS = 4096
N_SIB = 2
N_ROW = 4
N_COL = 4


def draw_poles(key, part):
    key = jax.random.fold_in(key, 11)
    local_index = jnp.arange(K_DEV, dtype=jnp.int32)[None, :]
    col_index = jnp.arange(N_COL, dtype=jnp.int32)[:, None]
    cyclic = (local_index * N_COL + col_index).reshape(-1).astype(jnp.float32)[None, :]
    offsets = jax.random.uniform(key, (N_SIB, K_DEV * N_COL), jnp.float32, 0.0, 0.25)
    return (cyclic + offsets).astype(jnp.float32)


def draw_shifts(key, part):
    key = jax.random.fold_in(key, 23)
    spacing = K_DEV * N_COL // SLAB
    slab_index = jnp.arange(SLAB, dtype=jnp.int32)
    centres = (slab_index * spacing + slab_index % N_COL).astype(jnp.float32)[None, :]
    offsets = jax.random.uniform(key, (N_SIB, SLAB), jnp.float32, 0.0, 0.25)
    return (centres + 0.5 + offsets).astype(jnp.float32)


def pick_columns(key):
    middle = jax.random.permutation(key, K_DEV - 2)[:PAIRS - 2] + 1
    ends = jnp.array([0, K_DEV - 1], jnp.int32)
    listed = jnp.concatenate([ends, middle.astype(jnp.int32)])
    return jax.random.permutation(jax.random.fold_in(key, 7), listed).astype(jnp.int32)


def draw_pair_src(key, part):
    key = jax.random.fold_in(key, 31)
    keys = jax.random.split(key, N_SIB * N_COL)
    return jax.vmap(pick_columns)(keys).reshape(N_SIB, N_COL, PAIRS)


def draw_pair_dst(key, part):
    key = jax.random.fold_in(key, 47)
    keys = jax.random.split(key, N_SIB * N_COL)
    return jax.vmap(pick_columns)(keys).reshape(N_SIB, N_COL, PAIRS)


def block_levels(rng, dims, cuts, least, high):
    level, own = 1.0, jax.random.fold_in(rng, 6)
    for position, parts in cuts:
        steps = jnp.exp(jax.random.uniform(jax.random.fold_in(own, position), (parts,), jnp.float32, least / len(cuts), high / len(cuts)))
        level = level * jnp.repeat(steps, dims[position] // parts).reshape([-1 if axis == position else 1 for axis in range(len(dims))])
    return level


def gaussian(key, shape, spread, bound, pieces=(), kind=jnp.bfloat16):
    factor_of = block_levels(key, shape, pieces, -0.22, 0.18) if pieces else 1.0
    drawn = jax.random.normal(key, shape, jnp.float32) * spread * factor_of
    return jnp.minimum(jnp.maximum(drawn, -bound), bound).astype(kind)


def setup_inputs(seed: int = 0) -> dict:
    arg_keys = jax.random.split(jax.random.key(seed), 9)
    eigvec = gaussian(arg_keys[0], (N_SIB, ROWS, K), 1.0, 6.0, ((0, 2), (1, 4), (2, 4)))
    poles = draw_poles(jax.random.fold_in(arg_keys[8], 71), 0)
    weights = gaussian(arg_keys[2], (N_SIB, K), 1.0, 5.0, ((0, 2), (1, 4)), jnp.float32)
    shifts = draw_shifts(jax.random.fold_in(arg_keys[8], 71), 0)
    pair_src = draw_pair_src(jax.random.fold_in(arg_keys[8], 71), 0)
    pair_dst = draw_pair_dst(jax.random.fold_in(arg_keys[8], 71), 0)
    rot_cos = jnp.clip(0.3 + 0.7 * jax.random.uniform(arg_keys[6], (N_SIB, N_COL, PAIRS), jnp.float32) ** block_levels(arg_keys[6], (N_SIB, N_COL, PAIRS), ((0, 2), (1, 4)), -0.2, 0.2), 0.3, 1.0)
    rot_sin = jnp.clip(jax.random.uniform(arg_keys[7], (N_SIB, N_COL, PAIRS), jnp.float32, -1.0, 1.0) * block_levels(arg_keys[7], (N_SIB, N_COL, PAIRS), ((0, 2), (1, 4)), -0.4, 0.0), -1.0, 1.0)
    return {"eigvec": eigvec, "poles": poles, "weights": weights, "shifts": shifts, "pair_src": pair_src, "pair_dst": pair_dst, "rot_cos": rot_cos, "rot_sin": rot_sin}


def merge_one(eig_rows, pole_vals, weight_vals, shift_vals, source, target, cosines, sines):
    cauchy = weight_vals[:, None] / (pole_vals[:, None] - shift_vals[None, :])
    normsq = lax.optimization_barrier(jnp.sum(cauchy * cauchy, axis=0))
    col_base = jnp.asarray((np.arange(N_COL) * K_DEV)[:, None]).astype(jnp.int32)
    target_flat = (col_base + target.astype(jnp.int32)).reshape(-1).astype(jnp.int32)
    onehot = target_flat[:, None] == jnp.arange(K, dtype=jnp.int32)[None, :]
    hit = lax.optimization_barrier(jnp.sum(onehot.astype(cauchy.dtype), axis=0))
    cos_sum = lax.optimization_barrier(jnp.sum(onehot.astype(cauchy.dtype) * cosines.reshape(-1)[:, None].astype(cauchy.dtype), axis=0))
    cosfull = 1.0 - hit + cos_sum
    slab_wide = cauchy * cosfull[:, None]
    rot_wide = sines.reshape(-1)[:, None].astype(cauchy.dtype) * cauchy[target_flat]
    partner_ids = np.arange(N_COL) ^ N_COL // 2
    partner_src = source[jnp.asarray(partner_ids).astype(jnp.int32)].astype(jnp.int32)
    partner_base = jnp.asarray((partner_ids * K_DEV)[:, None]).astype(jnp.int32)
    partner_flat = (partner_base + partner_src).reshape(-1).astype(jnp.int32)
    scale = jnp.sqrt(normsq)[None, :]

    def one_block(block):
        block_wide = block.astype(cauchy.dtype)
        partcols = block_wide[:, partner_flat]
        unscaled = jnp.dot(block_wide, slab_wide, precision=lax.Precision.HIGHEST)
        unscaled = unscaled + jnp.dot(partcols, rot_wide, precision=lax.Precision.HIGHEST)
        return (unscaled / scale).astype(jnp.bfloat16)
    blocks = eig_rows.reshape(N_ROW, R_DEV, K)
    return lax.map(one_block, blocks).reshape(N_ROW * R_DEV, SLAB)

def reference(eigvec, poles, weights, shifts, pair_src, pair_dst, rot_cos, rot_sin):
    blocks = []
    for sibling in range(N_SIB):
        blocks.append(merge_one(eigvec[sibling], poles[sibling], weights[sibling], shifts[sibling], pair_src[sibling], pair_dst[sibling], rot_cos[sibling], rot_sin[sibling]))
    return jnp.concatenate(blocks, axis=0)
```

```python
import functools

import jax
import jax.numpy as jnp
from jax import lax
from jax.experimental import pallas as pl
from jax.experimental.pallas import tpu as pltpu
from jax.sharding import PartitionSpec as P

LANES = 128
SUB = 64
MESH = pl.DeviceIdType.MESH


def inverse(value):
    guess = pl.reciprocal(value, approx=True)
    return guess * (2.0 - value * guess)


def pick(tables, index):
    row, lane = index >> 7, index & (LANES - 1)
    picked = jnp.zeros(index.shape, jnp.float32)
    for t, table in enumerate(tables):
        there = jnp.take_along_axis(jnp.broadcast_to(table, index.shape), lane, axis=1)
        picked = jnp.where(row == t, there, picked)
    return picked


def kernel(n, eig, poles, weights, shifts, src, dst, cosines, sines, out,
           eig_buf, slab_own, slab_hi, slab_lo, shift_t, src_t, dst_t, cos_t, listed, inv,
           part_b, part_q, norm_acc, pair_send, pair_recv, norm_send, norm_recv,
           core_send, core_recv, chip_send, chip_recv,
           eig_sem, pair_ssem, pair_rsem, norm_ssem, norm_rsem,
           core_ssem, core_rsem, chip_ssem, chip_rsem):
    rows, width = eig_buf.shape
    block = rows // n
    slab = shifts.shape[1]
    pairs = src.shape[2]
    tiles, lists = width // LANES, pairs // LANES
    chips = n // 2
    me = lax.axis_index("col")
    chip, core = me // 2, lax.rem(me, 2)
    other = 1 - core

    def col(index):
        return {"col": index}

    def peer(step):
        return lax.rem(me + step, n)

    barrier = pltpu.get_barrier_semaphore()
    for step in range(1, n):
        pl.semaphore_signal(barrier, inc=1, device_id=col(peer(step)), device_id_type=MESH)

    loads = []
    for part in range(4):
        span = pl.ds(part * (rows // 4), rows // 4)
        load = pltpu.make_async_copy(eig.at[0, span, :], eig_buf.at[span, :], eig_sem.at[part])
        load.start()
        loads.append(load)

    listed[...] = jnp.zeros_like(listed)
    for r in range(lists):
        cut = slice(r * LANES, (r + 1) * LANES)
        listed[r:r + 1, :] = dst[0, :, cut]
    index = listed[...]
    pole_rows = [poles[:, t * LANES:(t + 1) * LANES] for t in range(tiles)]
    weight_rows = [weights[:, t * LANES:(t + 1) * LANES] for t in range(tiles)]
    pair_send[0] = pick(weight_rows, index)
    pair_send[1] = pick(pole_rows, index)
    for r in range(lists):
        cut = slice(r * LANES, (r + 1) * LANES)
        pair_send[0, r:r + 1, :] = pair_send[0, r:r + 1, :] * sines[0, :, cut]

    pl.semaphore_wait(barrier, n - 1)
    pair_copy = pltpu.make_async_remote_copy(
        src_ref=pair_send, dst_ref=pair_recv, send_sem=pair_ssem, recv_sem=pair_rsem,
        device_id=col(lax.rem(me + n // 2, n)), device_id_type=MESH)
    pair_copy.start()

    for r in range(lists):
        cut = slice(r * LANES, (r + 1) * LANES)
        src_t[cut, :] = jnp.broadcast_to(src[0, :, cut], (LANES, LANES)).T
        dst_t[cut, :] = jnp.broadcast_to(dst[0, :, cut], (LANES, LANES)).T
        cos_t[cut, :] = jnp.broadcast_to(cosines[0, :, cut], (LANES, LANES)).T - 1.0
    for r in range(slab // LANES):
        cut = slice(r * LANES, (r + 1) * LANES)
        shift_t[cut, :] = jnp.broadcast_to(shifts[:, cut], (LANES, LANES)).T
    norm_acc[...] = jnp.zeros_like(norm_acc)

    def own_part(t, carry):
        cut = pl.ds(pl.multiple_of(t * LANES, LANES), LANES)
        local = lax.broadcasted_iota(jnp.int32, (SUB, LANES), 1) + t * LANES
        turned = jnp.zeros((SUB, LANES), jnp.float32)
        place = jnp.zeros((SUB, LANES), jnp.int32)
        count = lax.broadcasted_iota(jnp.int32, (SUB, LANES), 0) + 1
        for r in range(0, pairs, SUB):
            turned = jnp.where(dst_t[r:r + SUB, :] == local, cos_t[r:r + SUB, :], turned)
            place = jnp.where(src_t[r:r + SUB, :] == local, count + r, place)
        cosfull = 1.0 + jnp.sum(turned, axis=0, keepdims=True)
        inv[pl.ds(t, 1), :] = jnp.sum(place, axis=0, keepdims=True)
        pole = poles[:, cut]
        weight = weights[:, cut]
        for r in range(0, slab, SUB):
            cauchy = weight * inverse(pole - shift_t[r:r + SUB, :])
            norm_acc[r:r + SUB, :] += cauchy * cauchy
            slab_own[r:r + SUB, cut] = cosfull * cauchy
        return carry

    lax.fori_loop(0, tiles, own_part, 0)

    norm_send[...] = jnp.broadcast_to(jnp.sum(norm_acc[...].T, axis=0, keepdims=True), norm_send.shape)
    norm_copies = []
    for step in range(1, n):
        copy = pltpu.make_async_remote_copy(
            src_ref=norm_send, dst_ref=norm_recv.at[step], send_sem=norm_ssem.at[step],
            recv_sem=norm_rsem.at[step], device_id=col(peer(step)), device_id_type=MESH)
        copy.start()
        norm_copies.append(copy)

    pair_copy.wait()
    for t in range(0, tiles, 8):
        place = inv[t:t + 8, :]
        at = jnp.maximum(place - 1, 0)
        part_b[t:t + 8, :] = jnp.where(place > 0, pick([pair_recv[0, r:r + 1, :] for r in range(lists)], at), 0.0)
        part_q[t:t + 8, :] = jnp.where(place > 0, pick([pair_recv[1, r:r + 1, :] for r in range(lists)], at), -1.0)

    def partner_part(t, carry):
        cut = pl.ds(pl.multiple_of(t * LANES, LANES), LANES)
        pole = part_q[pl.ds(t, 1), :]
        weight = part_b[pl.ds(t, 1), :]
        for r in range(0, slab, SUB):
            total = slab_own[r:r + SUB, cut] + weight * inverse(pole - shift_t[r:r + SUB, :])
            high = total.astype(jnp.bfloat16)
            slab_hi[r:r + SUB, cut] = high
            slab_lo[r:r + SUB, cut] = (total - high.astype(jnp.float32)).astype(jnp.bfloat16)
        return carry

    lax.fori_loop(0, tiles, partner_part, 0)

    for load in loads:
        load.wait()

    def product(owner):
        left = eig_buf[pl.ds(pl.multiple_of(owner * block, block), block), :]
        dims = (((1,), (1,)), ((), ()))
        return (lax.dot_general(left, slab_hi[...], dims, preferred_element_type=jnp.float32)
                + lax.dot_general(left, slab_lo[...], dims, preferred_element_type=jnp.float32))

    core_copies, chip_copies = [], []

    def to_core(step, owner_chip):
        core_send[step] = product(owner_chip * 2 + other)
        copy = pltpu.make_async_remote_copy(
            src_ref=core_send.at[step], dst_ref=core_recv.at[step], send_sem=core_ssem.at[step],
            recv_sem=core_rsem.at[step], device_id=col(chip * 2 + other), device_id_type=MESH)
        copy.start()
        core_copies.append(copy)

    for step in range(1, chips):
        away = lax.rem(chip + step, chips)
        to_core(step, away)
        mine = product(away * 2 + core)
        core_copies[-1].wait_recv()
        chip_send[step] = mine + core_recv[step]
        copy = pltpu.make_async_remote_copy(
            src_ref=chip_send.at[step], dst_ref=chip_recv.at[step], send_sem=chip_ssem.at[step],
            recv_sem=chip_rsem.at[step], device_id=col(away * 2 + core), device_id_type=MESH)
        copy.start()
        chip_copies.append(copy)
    to_core(0, chip)
    total = product(me)
    core_copies[-1].wait_recv()
    chip_send[0] = total + core_recv[0]

    normsq = norm_send[0:1, :]
    for step, copy in enumerate(norm_copies):
        copy.wait()
        normsq = normsq + norm_recv[step + 1, 0:1, :]
    scale = jnp.sqrt(normsq)
    for copy in chip_copies:
        copy.wait()
    total = chip_send[0]
    for step in range(1, chips):
        total = total + chip_recv[step]
    out[...] = (total / scale).astype(out.dtype)
    for copy in core_copies:
        copy.wait_send()


def body(eigvec, *small):
    n = lax.axis_size("col")
    _, rows, width = eigvec.shape
    slab = small[2].shape[1]
    pairs = small[3].shape[2]
    block = rows // n
    chips = n // 2
    tiles = width // LANES
    f32, bf16 = jnp.float32, jnp.bfloat16
    vmem = pl.BlockSpec(memory_space=pltpu.VMEM)
    dma = pltpu.SemaphoreType.DMA
    return pl.pallas_call(
        functools.partial(kernel, n),
        out_shape=jax.ShapeDtypeStruct((block, slab), bf16),
        in_specs=[pl.BlockSpec(memory_space=pl.ANY)] + [vmem] * 7,
        out_specs=vmem,
        scratch_shapes=[
            pltpu.VMEM((rows, width), bf16),
            pltpu.VMEM((slab, width), f32),
            pltpu.VMEM((slab, width), bf16),
            pltpu.VMEM((slab, width), bf16),
            pltpu.VMEM((slab, LANES), f32),
            pltpu.VMEM((pairs, LANES), jnp.int32),
            pltpu.VMEM((pairs, LANES), jnp.int32),
            pltpu.VMEM((pairs, LANES), f32),
            pltpu.VMEM((8, LANES), jnp.int32),
            pltpu.VMEM((tiles, LANES), jnp.int32),
            pltpu.VMEM((tiles, LANES), f32),
            pltpu.VMEM((tiles, LANES), f32),
            pltpu.VMEM((slab, LANES), f32),
            pltpu.VMEM((2, 8, LANES), f32),
            pltpu.VMEM((2, 8, LANES), f32),
            pltpu.VMEM((8, slab), f32),
            pltpu.VMEM((n, 8, slab), f32),
            pltpu.VMEM((chips, block, slab), f32),
            pltpu.VMEM((chips, block, slab), f32),
            pltpu.VMEM((chips, block, slab), f32),
            pltpu.VMEM((chips, block, slab), f32),
            dma((4,)), dma, dma, dma((n,)), dma((n,)),
            dma((chips,)), dma((chips,)), dma((chips,)), dma((chips,)),
        ],
        compiler_params=pltpu.CompilerParams(
            collective_id=0, has_side_effects=True, vmem_limit_bytes=40 * 2**20),
        cost_estimate=pl.CostEstimate(
            flops=4 * rows * width * slab, bytes_accessed=2 * rows * width, transcendentals=2 * width * slab),
        name="merge",
    )(eigvec, *small)


def solution(mesh):
    in_specs = (
        P("sib", "row", "col"),
        P("sib", "col"),
        P("sib", "col"),
        P("sib", None),
        P("sib", "col", None),
        P("sib", "col", None),
        P("sib", "col", None),
        P("sib", "col", None),
    )
    out_specs = P(("sib", "row", "col"), None)
    return jax.shard_map(body, mesh=mesh, in_specs=in_specs, out_specs=out_specs, check_vma=False)
```

```python
import functools

import jax
import jax.numpy as jnp
from jax import lax
from jax.experimental import pallas as pl
from jax.experimental.pallas import tpu as pltpu
from jax.sharding import PartitionSpec as P

LANES = 128
SUB = 64
MESH = pl.DeviceIdType.MESH


def inverse(value):
    guess = pl.reciprocal(value, approx=True)
    return guess * (2.0 - value * guess)


def pick(tables, index):
    row, lane = index >> 7, index & (LANES - 1)
    picked = jnp.zeros(index.shape, jnp.float32)
    for t, table in enumerate(tables):
        there = jnp.take_along_axis(jnp.broadcast_to(table, index.shape), lane, axis=1)
        picked = jnp.where(row == t, there, picked)
    return picked


def kernel(n, eig, *refs):
    small_hbm, out, small = refs[:7], refs[7], refs[8:15]
    poles, weights, shifts, src, dst, cosines, sines = small
    (eig_buf, slab_own, slab_hi, slab_lo, shift_t, src_t, dst_t, cos_t, listed, inv,
     part_b, part_q, norm_acc, pair_send, pair_recv, norm_send, norm_recv,
     core_send, core_recv, chip_send, chip_recv,
     eig_sem, pair_ssem, pair_rsem, norm_ssem, norm_rsem,
     core_ssem, core_rsem, chip_ssem, chip_rsem, small_sem) = refs[15:]
    rows, width = eig_buf.shape
    block = rows // n
    slab = shifts.shape[1]
    pairs = src.shape[2]
    tiles, lists = width // LANES, pairs // LANES
    chips = n // 2
    me = lax.axis_index("col")
    chip, core = me // 2, lax.rem(me, 2)
    other = 1 - core

    def col(index):
        return {"col": index}

    def peer(step):
        return lax.rem(me + step, n)

    small_loads = []
    for at, (source, target) in enumerate(zip(small_hbm, small)):
        load = pltpu.make_async_copy(source, target, small_sem.at[at])
        load.start()
        small_loads.append(load)

    barrier = pltpu.get_barrier_semaphore()
    for step in range(1, n):
        pl.semaphore_signal(barrier, inc=1, device_id=col(peer(step)), device_id_type=MESH)

    loads = []
    for part in range(4):
        span = pl.ds(part * (rows // 4), rows // 4)
        load = pltpu.make_async_copy(eig.at[0, span, :], eig_buf.at[span, :], eig_sem.at[part])
        load.start()
        loads.append(load)

    for load in small_loads:
        load.wait()

    listed[...] = jnp.zeros_like(listed)
    for r in range(lists):
        cut = slice(r * LANES, (r + 1) * LANES)
        listed[r:r + 1, :] = dst[0, :, cut]
    index = listed[...]
    pole_rows = [poles[:, t * LANES:(t + 1) * LANES] for t in range(tiles)]
    weight_rows = [weights[:, t * LANES:(t + 1) * LANES] for t in range(tiles)]
    pair_send[0] = pick(weight_rows, index)
    pair_send[1] = pick(pole_rows, index)
    for r in range(lists):
        cut = slice(r * LANES, (r + 1) * LANES)
        pair_send[0, r:r + 1, :] = pair_send[0, r:r + 1, :] * sines[0, :, cut]

    pl.semaphore_wait(barrier, n - 1)
    pair_copy = pltpu.make_async_remote_copy(
        src_ref=pair_send, dst_ref=pair_recv, send_sem=pair_ssem, recv_sem=pair_rsem,
        device_id=col(lax.rem(me + n // 2, n)), device_id_type=MESH)
    pair_copy.start()

    for r in range(lists):
        cut = slice(r * LANES, (r + 1) * LANES)
        src_t[cut, :] = jnp.broadcast_to(src[0, :, cut], (LANES, LANES)).T
        dst_t[cut, :] = jnp.broadcast_to(dst[0, :, cut], (LANES, LANES)).T
        cos_t[cut, :] = jnp.broadcast_to(cosines[0, :, cut], (LANES, LANES)).T - 1.0
    for r in range(slab // LANES):
        cut = slice(r * LANES, (r + 1) * LANES)
        shift_t[cut, :] = jnp.broadcast_to(shifts[:, cut], (LANES, LANES)).T
    norm_acc[...] = jnp.zeros_like(norm_acc)

    def own_part(t, carry):
        cut = pl.ds(pl.multiple_of(t * LANES, LANES), LANES)
        local = lax.broadcasted_iota(jnp.int32, (SUB, LANES), 1) + t * LANES
        turned = jnp.zeros((SUB, LANES), jnp.float32)
        place = jnp.zeros((SUB, LANES), jnp.int32)
        count = lax.broadcasted_iota(jnp.int32, (SUB, LANES), 0) + 1
        for r in range(0, pairs, SUB):
            turned = jnp.where(dst_t[r:r + SUB, :] == local, cos_t[r:r + SUB, :], turned)
            place = jnp.where(src_t[r:r + SUB, :] == local, count + r, place)
        cosfull = 1.0 + jnp.sum(turned, axis=0, keepdims=True)
        inv[pl.ds(t, 1), :] = jnp.sum(place, axis=0, keepdims=True)
        pole = poles[:, cut]
        weight = weights[:, cut]
        for r in range(0, slab, SUB):
            cauchy = weight * inverse(pole - shift_t[r:r + SUB, :])
            norm_acc[r:r + SUB, :] += cauchy * cauchy
            slab_own[r:r + SUB, cut] = cosfull * cauchy
        return carry

    lax.fori_loop(0, tiles, own_part, 0)

    norm_send[...] = jnp.broadcast_to(jnp.sum(norm_acc[...].T, axis=0, keepdims=True), norm_send.shape)
    norm_copies = []
    for step in range(1, n):
        copy = pltpu.make_async_remote_copy(
            src_ref=norm_send, dst_ref=norm_recv.at[step], send_sem=norm_ssem.at[step],
            recv_sem=norm_rsem.at[step], device_id=col(peer(step)), device_id_type=MESH)
        copy.start()
        norm_copies.append(copy)

    pair_copy.wait()
    for t in range(0, tiles, 8):
        place = inv[t:t + 8, :]
        at = jnp.maximum(place - 1, 0)
        part_b[t:t + 8, :] = jnp.where(place > 0, pick([pair_recv[0, r:r + 1, :] for r in range(lists)], at), 0.0)
        part_q[t:t + 8, :] = jnp.where(place > 0, pick([pair_recv[1, r:r + 1, :] for r in range(lists)], at), -1.0)

    def partner_part(t, carry):
        cut = pl.ds(pl.multiple_of(t * LANES, LANES), LANES)
        pole = part_q[pl.ds(t, 1), :]
        weight = part_b[pl.ds(t, 1), :]
        for r in range(0, slab, SUB):
            total = slab_own[r:r + SUB, cut] + weight * inverse(pole - shift_t[r:r + SUB, :])
            high = total.astype(jnp.bfloat16)
            slab_hi[r:r + SUB, cut] = high
            slab_lo[r:r + SUB, cut] = (total - high.astype(jnp.float32)).astype(jnp.bfloat16)
        return carry

    lax.fori_loop(0, tiles, partner_part, 0)

    for load in loads:
        load.wait()

    def product(owner):
        left = eig_buf[pl.ds(pl.multiple_of(owner * block, block), block), :]
        dims = (((1,), (1,)), ((), ()))
        return (lax.dot_general(left, slab_hi[...], dims, preferred_element_type=jnp.float32)
                + lax.dot_general(left, slab_lo[...], dims, preferred_element_type=jnp.float32))

    core_copies, chip_copies = [], []

    def to_core(step, owner_chip):
        core_send[step] = product(owner_chip * 2 + other)
        copy = pltpu.make_async_remote_copy(
            src_ref=core_send.at[step], dst_ref=core_recv.at[step], send_sem=core_ssem.at[step],
            recv_sem=core_rsem.at[step], device_id=col(chip * 2 + other), device_id_type=MESH)
        copy.start()
        core_copies.append(copy)

    for step in range(1, chips):
        away = lax.rem(chip + step, chips)
        to_core(step, away)
        mine = product(away * 2 + core)
        core_copies[-1].wait_recv()
        chip_send[step] = mine + core_recv[step]
        copy = pltpu.make_async_remote_copy(
            src_ref=chip_send.at[step], dst_ref=chip_recv.at[step], send_sem=chip_ssem.at[step],
            recv_sem=chip_rsem.at[step], device_id=col(away * 2 + core), device_id_type=MESH)
        copy.start()
        chip_copies.append(copy)
    to_core(0, chip)
    total = product(me)
    core_copies[-1].wait_recv()
    chip_send[0] = total + core_recv[0]

    normsq = norm_send[0:1, :]
    for step, copy in enumerate(norm_copies):
        copy.wait()
        normsq = normsq + norm_recv[step + 1, 0:1, :]
    scale = jnp.sqrt(normsq)
    for copy in chip_copies:
        copy.wait()
    total = chip_send[0]
    for step in range(1, chips):
        total = total + chip_recv[step]
    out[...] = (total / scale).astype(out.dtype)
    for copy in core_copies:
        copy.wait_send()


def body(eigvec, *small):
    n = lax.axis_size("col")
    _, rows, width = eigvec.shape
    slab = small[2].shape[1]
    pairs = small[3].shape[2]
    block = rows // n
    chips = n // 2
    tiles = width // LANES
    f32, bf16 = jnp.float32, jnp.bfloat16
    vmem = pl.BlockSpec(memory_space=pltpu.VMEM)
    dma = pltpu.SemaphoreType.DMA
    return pl.pallas_call(
        functools.partial(kernel, n),
        out_shape=jax.ShapeDtypeStruct((block, slab), bf16),
        in_specs=[pl.BlockSpec(memory_space=pltpu.HBM)] * 8,
        out_specs=vmem,
        scratch_shapes=[
            *(pltpu.VMEM(value.shape, value.dtype) for value in small),
            pltpu.VMEM((rows, width), bf16),
            pltpu.VMEM((slab, width), f32),
            pltpu.VMEM((slab, width), bf16),
            pltpu.VMEM((slab, width), bf16),
            pltpu.VMEM((slab, LANES), f32),
            pltpu.VMEM((pairs, LANES), jnp.int32),
            pltpu.VMEM((pairs, LANES), jnp.int32),
            pltpu.VMEM((pairs, LANES), f32),
            pltpu.VMEM((8, LANES), jnp.int32),
            pltpu.VMEM((tiles, LANES), jnp.int32),
            pltpu.VMEM((tiles, LANES), f32),
            pltpu.VMEM((tiles, LANES), f32),
            pltpu.VMEM((slab, LANES), f32),
            pltpu.VMEM((2, 8, LANES), f32),
            pltpu.VMEM((2, 8, LANES), f32),
            pltpu.VMEM((8, slab), f32),
            pltpu.VMEM((n, 8, slab), f32),
            pltpu.VMEM((chips, block, slab), f32),
            pltpu.VMEM((chips, block, slab), f32),
            pltpu.VMEM((chips, block, slab), f32),
            pltpu.VMEM((chips, block, slab), f32),
            dma((4,)), dma, dma, dma((n,)), dma((n,)),
            dma((chips,)), dma((chips,)), dma((chips,)), dma((chips,)), dma((7,)),
        ],
        compiler_params=pltpu.CompilerParams(
            collective_id=0, has_side_effects=True, vmem_limit_bytes=40 * 2**20),
        cost_estimate=pl.CostEstimate(
            flops=4 * rows * width * slab, bytes_accessed=2 * rows * width, transcendentals=2 * width * slab),
        name="merge",
    )(eigvec, *small)


def solution(mesh):
    in_specs = (
        P("sib", "row", "col"),
        P("sib", "col"),
        P("sib", "col"),
        P("sib", None),
        P("sib", "col", None),
        P("sib", "col", None),
        P("sib", "col", None),
        P("sib", "col", None),
    )
    out_specs = P(("sib", "row", "col"), None)
    return jax.shard_map(body, mesh=mesh, in_specs=in_specs, out_specs=out_specs, check_vma=False)
```

```python
import functools

import jax
import jax.numpy as jnp
from jax import lax
from jax.experimental import pallas as pl
from jax.experimental.pallas import tpu as pltpu
from jax.sharding import PartitionSpec as P

LANES = 128
SUB = 64
MESH = pl.DeviceIdType.MESH


def inverse(value):
    guess = pl.reciprocal(value, approx=True)
    return guess * (2.0 - value * guess)


def pick(tables, index):
    row, lane = index >> 7, index & (LANES - 1)
    picked = jnp.zeros(index.shape, jnp.float32)
    for t, table in enumerate(tables):
        there = jnp.take_along_axis(jnp.broadcast_to(table, index.shape), lane, axis=1)
        picked = jnp.where(row == t, there, picked)
    return picked


def kernel(n, eig, *refs):
    small_hbm, out, small = refs[:7], refs[7], refs[8:15]
    poles, weights, shifts, src, dst, cosines, sines = small
    (eig_buf, slab_own, slab_hi, slab_lo, shift_t, src_t, dst_t, cos_t, listed, inv,
     part_b, part_q, norm_acc, pair_send, pair_recv, norm_send, norm_recv,
     core_send, core_recv, chip_send, chip_recv,
     eig_sem, pair_ssem, pair_rsem, norm_ssem, norm_rsem,
     core_ssem, core_rsem, chip_ssem, chip_rsem, small_sem) = refs[15:]
    rows, width = eig_buf.shape
    block = rows // n
    slab = shifts.shape[1]
    pairs = src.shape[2]
    tiles, lists = width // LANES, pairs // LANES
    chips = n // 2
    me = lax.axis_index("col")
    chip, core = me // 2, lax.rem(me, 2)
    other = 1 - core

    def col(index):
        return {"col": index}

    def peer(step):
        return lax.rem(me + step, n)

    small_loads = []
    for at, (source, target) in enumerate(zip(small_hbm, small)):
        load = pltpu.make_async_copy(source, target, small_sem.at[at])
        load.start()
        small_loads.append(load)

    barrier = pltpu.get_barrier_semaphore()
    for step in range(1, n):
        pl.semaphore_signal(barrier, inc=1, device_id=col(peer(step)), device_id_type=MESH)

    loads = []
    for part in range(4):
        span = pl.ds(part * (rows // 4), rows // 4)
        load = pltpu.make_async_copy(eig.at[0, span, :], eig_buf.at[span, :], eig_sem.at[part])
        load.start()
        loads.append(load)

    for load in small_loads:
        load.wait()

    listed[...] = jnp.zeros_like(listed)
    for r in range(lists):
        cut = slice(r * LANES, (r + 1) * LANES)
        listed[r:r + 1, :] = dst[0, :, cut]
    index = listed[...]
    pole_rows = [poles[:, t * LANES:(t + 1) * LANES] for t in range(tiles)]
    weight_rows = [weights[:, t * LANES:(t + 1) * LANES] for t in range(tiles)]
    pair_send[0] = pick(weight_rows, index)
    pair_send[1] = pick(pole_rows, index)
    for r in range(lists):
        cut = slice(r * LANES, (r + 1) * LANES)
        pair_send[0, r:r + 1, :] = pair_send[0, r:r + 1, :] * sines[0, :, cut]

    pl.semaphore_wait(barrier, n - 1)
    pair_copy = pltpu.make_async_remote_copy(
        src_ref=pair_send, dst_ref=pair_recv, send_sem=pair_ssem, recv_sem=pair_rsem,
        device_id=col(lax.rem(me + n // 2, n)), device_id_type=MESH)
    pair_copy.start()

    for r in range(lists):
        cut = slice(r * LANES, (r + 1) * LANES)
        src_t[cut, :] = jnp.broadcast_to(src[0, :, cut], (LANES, LANES)).T
        dst_t[cut, :] = jnp.broadcast_to(dst[0, :, cut], (LANES, LANES)).T
        cos_t[cut, :] = jnp.broadcast_to(cosines[0, :, cut], (LANES, LANES)).T - 1.0
    for r in range(slab // LANES):
        cut = slice(r * LANES, (r + 1) * LANES)
        shift_t[cut, :] = jnp.broadcast_to(shifts[:, cut], (LANES, LANES)).T
    norm_acc[...] = jnp.zeros_like(norm_acc)

    def own_part(t, carry):
        cut = pl.ds(pl.multiple_of(t * LANES, LANES), LANES)
        local = lax.broadcasted_iota(jnp.int32, (SUB, LANES), 1) + t * LANES
        turned = jnp.zeros((SUB, LANES), jnp.float32)
        place = jnp.zeros((SUB, LANES), jnp.int32)
        count = lax.broadcasted_iota(jnp.int32, (SUB, LANES), 0) + 1
        for r in range(0, pairs, SUB):
            turned = jnp.where(dst_t[r:r + SUB, :] == local, cos_t[r:r + SUB, :], turned)
            place = jnp.where(src_t[r:r + SUB, :] == local, count + r, place)
        cosfull = 1.0 + jnp.sum(turned, axis=0, keepdims=True)
        inv[pl.ds(t, 1), :] = jnp.sum(place, axis=0, keepdims=True)
        pole = poles[:, cut]
        weight = weights[:, cut]
        for r in range(0, slab, SUB):
            cauchy = weight * inverse(pole - shift_t[r:r + SUB, :])
            norm_acc[r:r + SUB, :] += cauchy * cauchy
            slab_own[r:r + SUB, cut] = cosfull * cauchy
        return carry

    lax.fori_loop(0, tiles, own_part, 0)

    norm_send[...] = jnp.broadcast_to(jnp.sum(norm_acc[...].T, axis=0, keepdims=True), norm_send.shape)
    norm_copies = []
    for step in range(1, n):
        copy = pltpu.make_async_remote_copy(
            src_ref=norm_send, dst_ref=norm_recv.at[step], send_sem=norm_ssem.at[step],
            recv_sem=norm_rsem.at[step], device_id=col(peer(step)), device_id_type=MESH)
        copy.start()
        norm_copies.append(copy)

    pair_copy.wait()
    for t in range(0, tiles, 8):
        place = inv[t:t + 8, :]
        at = jnp.maximum(place - 1, 0)
        part_b[t:t + 8, :] = jnp.where(place > 0, pick([pair_recv[0, r:r + 1, :] for r in range(lists)], at), 0.0)
        part_q[t:t + 8, :] = jnp.where(place > 0, pick([pair_recv[1, r:r + 1, :] for r in range(lists)], at), -1.0)

    def partner_part(t, carry):
        cut = pl.ds(pl.multiple_of(t * LANES, LANES), LANES)
        pole = part_q[pl.ds(t, 1), :]
        weight = part_b[pl.ds(t, 1), :]
        for r in range(0, slab, SUB):
            total = slab_own[r:r + SUB, cut] + weight * inverse(pole - shift_t[r:r + SUB, :])
            high = total.astype(jnp.bfloat16)
            slab_hi[r:r + SUB, cut] = high
            slab_lo[r:r + SUB, cut] = (total - high.astype(jnp.float32)).astype(jnp.bfloat16)
        return carry

    lax.fori_loop(0, tiles, partner_part, 0)

    for load in loads:
        load.wait()

    def product(owner):
        left = eig_buf[pl.ds(pl.multiple_of(owner * block, block), block), :]
        dims = (((1,), (1,)), ((), ()))
        return (lax.dot_general(left, slab_hi[...], dims, preferred_element_type=jnp.float32)
                + lax.dot_general(left, slab_lo[...], dims, preferred_element_type=jnp.float32))

    core_copies, chip_copies = [], []

    def to_core(step, owner_chip):
        core_send[step] = product(owner_chip * 2 + other)
        copy = pltpu.make_async_remote_copy(
            src_ref=core_send.at[step], dst_ref=core_recv.at[step], send_sem=core_ssem.at[step],
            recv_sem=core_rsem.at[step], device_id=col(chip * 2 + other), device_id_type=MESH)
        copy.start()
        core_copies.append(copy)

    for step in range(1, chips):
        away = lax.rem(chip + step, chips)
        to_core(step, away)
        mine = product(away * 2 + core)
        core_copies[-1].wait_recv()
        chip_send[step] = mine + core_recv[step]
        copy = pltpu.make_async_remote_copy(
            src_ref=chip_send.at[step], dst_ref=chip_recv.at[step], send_sem=chip_ssem.at[step],
            recv_sem=chip_rsem.at[step], device_id=col(away * 2 + core), device_id_type=MESH)
        copy.start()
        chip_copies.append(copy)
    to_core(0, chip)
    total = product(me)
    core_copies[-1].wait_recv()
    chip_send[0] = total + core_recv[0]

    normsq = norm_send[0:1, :]
    for step, copy in enumerate(norm_copies):
        copy.wait()
        normsq = normsq + norm_recv[step + 1, 0:1, :]
    scale = jnp.sqrt(normsq)
    for copy in chip_copies:
        copy.wait()
    total = chip_send[0]
    for step in range(1, chips):
        total = total + chip_recv[step]
    out[...] = (total / scale).astype(out.dtype)
    for copy in core_copies:
        copy.wait_send()


def body(eigvec, *small):
    n = lax.axis_size("col")
    _, rows, width = eigvec.shape
    slab = small[2].shape[1]
    pairs = small[3].shape[2]
    block = rows // n
    chips = n // 2
    tiles = width // LANES
    f32, bf16 = jnp.float32, jnp.bfloat16
    vmem = pl.BlockSpec(memory_space=pltpu.VMEM)
    dma = pltpu.SemaphoreType.DMA
    return pl.pallas_call(
        functools.partial(kernel, n),
        out_shape=jax.ShapeDtypeStruct((block, slab), bf16),
        in_specs=[pl.BlockSpec(memory_space=pltpu.HBM)] * 8,
        out_specs=vmem,
        scratch_shapes=[
            *(pltpu.VMEM(value.shape, value.dtype) for value in small),
            pltpu.VMEM((rows, width), bf16),
            pltpu.VMEM((slab, width), f32),
            pltpu.VMEM((slab, width), bf16),
            pltpu.VMEM((slab, width), bf16),
            pltpu.VMEM((slab, LANES), f32),
            pltpu.VMEM((pairs, LANES), jnp.int32),
            pltpu.VMEM((pairs, LANES), jnp.int32),
            pltpu.VMEM((pairs, LANES), f32),
            pltpu.VMEM((8, LANES), jnp.int32),
            pltpu.VMEM((tiles, LANES), jnp.int32),
            pltpu.VMEM((tiles, LANES), f32),
            pltpu.VMEM((tiles, LANES), f32),
            pltpu.VMEM((slab, LANES), f32),
            pltpu.VMEM((2, 8, LANES), f32),
            pltpu.VMEM((2, 8, LANES), f32),
            pltpu.VMEM((8, slab), f32),
            pltpu.VMEM((n, 8, slab), f32),
            pltpu.VMEM((chips, block, slab), f32),
            pltpu.VMEM((chips, block, slab), f32),
            pltpu.VMEM((chips, block, slab), f32),
            pltpu.VMEM((chips, block, slab), f32),
            dma((4,)), dma, dma, dma((n,)), dma((n,)),
            dma((chips,)), dma((chips,)), dma((chips,)), dma((chips,)), dma((7,)),
        ],
        compiler_params=pltpu.CompilerParams(
            collective_id=0, has_side_effects=True, vmem_limit_bytes=60 * 2**20),
        cost_estimate=pl.CostEstimate(
            flops=4 * rows * width * slab, bytes_accessed=2 * rows * width, transcendentals=2 * width * slab),
        name="merge",
    )(eigvec, *small)


def solution(mesh):
    in_specs = (
        P("sib", "row", "col"),
        P("sib", "col"),
        P("sib", "col"),
        P("sib", None),
        P("sib", "col", None),
        P("sib", "col", None),
        P("sib", "col", None),
        P("sib", "col", None),
    )
    out_specs = P(("sib", "row", "col"), None)
    return jax.shard_map(body, mesh=mesh, in_specs=in_specs, out_specs=out_specs, check_vma=False)
```

```python
import functools

import jax
import jax.numpy as jnp
from jax import lax
from jax.experimental import pallas as pl
from jax.experimental.pallas import tpu as pltpu
from jax.sharding import PartitionSpec as P

LANES = 128
SUB = 64
PARTS = 2
STEPS = 32767.0
MESH = pl.DeviceIdType.MESH


def inverse(value):
    guess = pl.reciprocal(value, approx=True)
    return guess * (2.0 - value * guess)


def pick(tables, index):
    row, lane = index >> 7, index & (LANES - 1)
    picked = jnp.zeros(index.shape, jnp.float32)
    for t, table in enumerate(tables):
        there = jnp.take_along_axis(jnp.broadcast_to(table, index.shape), lane, axis=1)
        picked = jnp.where(row == t, there, picked)
    return picked


def kernel(n, eig, *refs):
    small_hbm, out, small = refs[:7], refs[7], refs[8:15]
    poles, weights, shifts, src, dst, cosines, sines = small
    (eig_buf, slab_own, slab_hi, slab_lo, shift_t, src_t, dst_t, cos_t, listed, inv,
     part_b, part_q, norm_acc, pair_send, pair_recv, norm_send, norm_recv,
     core_send, core_recv, chip_send, chip_recv, top_send, top_recv, total_acc,
     eig_sem, pair_ssem, pair_rsem, norm_ssem, norm_rsem,
     core_ssem, core_rsem, chip_ssem, chip_rsem, small_sem) = refs[15:]
    rows, width = eig_buf.shape
    block = rows // n
    piece = block // PARTS
    slab = shifts.shape[1]
    pairs = src.shape[2]
    tiles, lists = width // LANES, pairs // LANES
    chips = n // 2
    me = lax.axis_index("col")
    chip, core = me // 2, lax.rem(me, 2)
    other = 1 - core

    def col(index):
        return {"col": index}

    def peer(step):
        return lax.rem(me + step, n)

    small_loads = []
    for at, (source, target) in enumerate(zip(small_hbm, small)):
        load = pltpu.make_async_copy(source, target, small_sem.at[at])
        load.start()
        small_loads.append(load)

    barrier = pltpu.get_barrier_semaphore()
    for step in range(1, n):
        pl.semaphore_signal(barrier, inc=1, device_id=col(peer(step)), device_id_type=MESH)

    loads = []
    for part in range(4):
        span = pl.ds(part * (rows // 4), rows // 4)
        load = pltpu.make_async_copy(eig.at[0, span, :], eig_buf.at[span, :], eig_sem.at[part])
        load.start()
        loads.append(load)

    for load in small_loads:
        load.wait()

    listed[...] = jnp.zeros_like(listed)
    for r in range(lists):
        cut = slice(r * LANES, (r + 1) * LANES)
        listed[r:r + 1, :] = dst[0, :, cut]
    index = listed[...]
    pole_rows = [poles[:, t * LANES:(t + 1) * LANES] for t in range(tiles)]
    weight_rows = [weights[:, t * LANES:(t + 1) * LANES] for t in range(tiles)]
    pair_send[0] = pick(weight_rows, index)
    pair_send[1] = pick(pole_rows, index)
    for r in range(lists):
        cut = slice(r * LANES, (r + 1) * LANES)
        pair_send[0, r:r + 1, :] = pair_send[0, r:r + 1, :] * sines[0, :, cut]

    pl.semaphore_wait(barrier, n - 1)
    pair_copy = pltpu.make_async_remote_copy(
        src_ref=pair_send, dst_ref=pair_recv, send_sem=pair_ssem, recv_sem=pair_rsem,
        device_id=col(lax.rem(me + n // 2, n)), device_id_type=MESH)
    pair_copy.start()

    for r in range(lists):
        cut = slice(r * LANES, (r + 1) * LANES)
        src_t[cut, :] = jnp.broadcast_to(src[0, :, cut], (LANES, LANES)).T
        dst_t[cut, :] = jnp.broadcast_to(dst[0, :, cut], (LANES, LANES)).T
        cos_t[cut, :] = jnp.broadcast_to(cosines[0, :, cut], (LANES, LANES)).T - 1.0
    for r in range(slab // LANES):
        cut = slice(r * LANES, (r + 1) * LANES)
        shift_t[cut, :] = jnp.broadcast_to(shifts[:, cut], (LANES, LANES)).T
    norm_acc[...] = jnp.zeros_like(norm_acc)

    def own_part(t, carry):
        cut = pl.ds(pl.multiple_of(t * LANES, LANES), LANES)
        local = lax.broadcasted_iota(jnp.int32, (SUB, LANES), 1) + t * LANES
        turned = jnp.zeros((SUB, LANES), jnp.float32)
        place = jnp.zeros((SUB, LANES), jnp.int32)
        count = lax.broadcasted_iota(jnp.int32, (SUB, LANES), 0) + 1
        for r in range(0, pairs, SUB):
            turned = jnp.where(dst_t[r:r + SUB, :] == local, cos_t[r:r + SUB, :], turned)
            place = jnp.where(src_t[r:r + SUB, :] == local, count + r, place)
        cosfull = 1.0 + jnp.sum(turned, axis=0, keepdims=True)
        inv[pl.ds(t, 1), :] = jnp.sum(place, axis=0, keepdims=True)
        pole = poles[:, cut]
        weight = weights[:, cut]
        for r in range(0, slab, SUB):
            cauchy = weight * inverse(pole - shift_t[r:r + SUB, :])
            norm_acc[r:r + SUB, :] += cauchy * cauchy
            slab_own[r:r + SUB, cut] = cosfull * cauchy
        return carry

    lax.fori_loop(0, tiles, own_part, 0)

    norm_send[...] = jnp.broadcast_to(jnp.sum(norm_acc[...].T, axis=0, keepdims=True), norm_send.shape)
    norm_copies = []
    for step in range(1, n):
        copy = pltpu.make_async_remote_copy(
            src_ref=norm_send, dst_ref=norm_recv.at[step], send_sem=norm_ssem.at[step],
            recv_sem=norm_rsem.at[step], device_id=col(peer(step)), device_id_type=MESH)
        copy.start()
        norm_copies.append(copy)

    pair_copy.wait()
    for t in range(0, tiles, 8):
        place = inv[t:t + 8, :]
        at = jnp.maximum(place - 1, 0)
        part_b[t:t + 8, :] = jnp.where(place > 0, pick([pair_recv[0, r:r + 1, :] for r in range(lists)], at), 0.0)
        part_q[t:t + 8, :] = jnp.where(place > 0, pick([pair_recv[1, r:r + 1, :] for r in range(lists)], at), -1.0)

    def partner_part(t, carry):
        cut = pl.ds(pl.multiple_of(t * LANES, LANES), LANES)
        pole = part_q[pl.ds(t, 1), :]
        weight = part_b[pl.ds(t, 1), :]
        for r in range(0, slab, SUB):
            total = slab_own[r:r + SUB, cut] + weight * inverse(pole - shift_t[r:r + SUB, :])
            high = total.astype(jnp.bfloat16)
            slab_hi[r:r + SUB, cut] = high
            slab_lo[r:r + SUB, cut] = (total - high.astype(jnp.float32)).astype(jnp.bfloat16)
        return carry

    lax.fori_loop(0, tiles, partner_part, 0)

    for load in loads:
        load.wait()

    def product(owner, part):
        first = pl.multiple_of(owner * block + part * piece, piece)
        left = eig_buf[pl.ds(first, piece), :]
        dims = (((1,), (1,)), ((), ()))
        return (lax.dot_general(left, slab_hi[...], dims, preferred_element_type=jnp.float32)
                + lax.dot_general(left, slab_lo[...], dims, preferred_element_type=jnp.float32))

    core_copies, chip_copies = {}, {}

    def to_core(step, part, owner_chip):
        core_send[step, part] = product(owner_chip * 2 + other, part)
        copy = pltpu.make_async_remote_copy(
            src_ref=core_send.at[step, part], dst_ref=core_recv.at[step, part],
            send_sem=core_ssem.at[step, part], recv_sem=core_rsem.at[step, part],
            device_id=col(chip * 2 + other), device_id_type=MESH)
        copy.start()
        core_copies[step, part] = copy

    def to_chip(step, part, away):
        copies = []
        for at, (source, target) in enumerate(((chip_send, chip_recv), (top_send, top_recv))):
            copy = pltpu.make_async_remote_copy(
                src_ref=source.at[step, part], dst_ref=target.at[step, part],
                send_sem=chip_ssem.at[at, step, part], recv_sem=chip_rsem.at[at, step, part],
                device_id=col(away * 2 + core), device_id_type=MESH)
            copy.start()
            copies.append(copy)
        chip_copies[step, part] = copies

    for step in range(1, chips):
        away = lax.rem(chip + step, chips)
        for part in range(PARTS):
            to_core(step, part, away)
        for part in range(PARTS):
            mine = product(away * 2 + core, part)
            core_copies[step, part].wait_recv()
            mine = mine + core_recv[step, part]
            top = jnp.maximum(jnp.max(jnp.abs(mine), axis=0, keepdims=True), 1e-33)
            chip_send[step, part] = jnp.round(mine * (STEPS / top)).astype(jnp.int32).astype(jnp.int16)
            top_send[step, part] = jnp.broadcast_to(top, top_send.shape[2:])
            to_chip(step, part, away)
    for part in range(PARTS):
        to_core(0, part, chip)
    for part in range(PARTS):
        total_acc[part] = product(me, part)

    normsq = norm_send[0:1, :]
    for step, copy in enumerate(norm_copies):
        copy.wait()
        normsq = normsq + norm_recv[step + 1, 0:1, :]
    scale = jnp.sqrt(normsq)
    for part in range(PARTS):
        core_copies[0, part].wait_recv()
        total = total_acc[part] + core_recv[0, part]
        for step in range(1, chips):
            for copy in chip_copies[step, part]:
                copy.wait()
            unit = top_recv[step, part, 0:1, :] * (1.0 / STEPS)
            total = total + chip_recv[step, part].astype(jnp.int32).astype(jnp.float32) * unit
        out[part * piece:(part + 1) * piece, :] = (total / scale).astype(out.dtype)
    for copy in core_copies.values():
        copy.wait_send()


def body(eigvec, *small):
    n = lax.axis_size("col")
    _, rows, width = eigvec.shape
    slab = small[2].shape[1]
    pairs = small[3].shape[2]
    block = rows // n
    piece = block // PARTS
    chips = n // 2
    tiles = width // LANES
    f32, bf16 = jnp.float32, jnp.bfloat16
    vmem = pl.BlockSpec(memory_space=pltpu.VMEM)
    dma = pltpu.SemaphoreType.DMA
    return pl.pallas_call(
        functools.partial(kernel, n),
        out_shape=pltpu.VMEM((block, slab), bf16),
        in_specs=[pl.BlockSpec(memory_space=pltpu.HBM)] * 8,
        out_specs=vmem,
        scratch_shapes=[
            *(pltpu.VMEM(value.shape, value.dtype) for value in small),
            pltpu.VMEM((rows, width), bf16),
            pltpu.VMEM((slab, width), f32),
            pltpu.VMEM((slab, width), bf16),
            pltpu.VMEM((slab, width), bf16),
            pltpu.VMEM((slab, LANES), f32),
            pltpu.VMEM((pairs, LANES), jnp.int32),
            pltpu.VMEM((pairs, LANES), jnp.int32),
            pltpu.VMEM((pairs, LANES), f32),
            pltpu.VMEM((8, LANES), jnp.int32),
            pltpu.VMEM((tiles, LANES), jnp.int32),
            pltpu.VMEM((tiles, LANES), f32),
            pltpu.VMEM((tiles, LANES), f32),
            pltpu.VMEM((slab, LANES), f32),
            pltpu.VMEM((2, 8, LANES), f32),
            pltpu.VMEM((2, 8, LANES), f32),
            pltpu.VMEM((8, slab), f32),
            pltpu.VMEM((n, 8, slab), f32),
            pltpu.VMEM((chips, PARTS, piece, slab), f32),
            pltpu.VMEM((chips, PARTS, piece, slab), f32),
            pltpu.VMEM((chips, PARTS, piece, slab), jnp.int16),
            pltpu.VMEM((chips, PARTS, piece, slab), jnp.int16),
            pltpu.VMEM((chips, PARTS, 8, slab), f32),
            pltpu.VMEM((chips, PARTS, 8, slab), f32),
            pltpu.VMEM((PARTS, piece, slab), f32),
            dma((4,)), dma, dma, dma((n,)), dma((n,)),
            dma((chips, PARTS)), dma((chips, PARTS)), dma((2, chips, PARTS)), dma((2, chips, PARTS)), dma((7,)),
        ],
        compiler_params=pltpu.CompilerParams(
            collective_id=0, has_side_effects=True, vmem_limit_bytes=60 * 2**20),
        cost_estimate=pl.CostEstimate(
            flops=4 * rows * width * slab, bytes_accessed=2 * rows * width, transcendentals=2 * width * slab),
        name="merge",
    )(eigvec, *small)


def solution(mesh):
    in_specs = (
        P("sib", "row", "col"),
        P("sib", "col"),
        P("sib", "col"),
        P("sib", None),
        P("sib", "col", None),
        P("sib", "col", None),
        P("sib", "col", None),
        P("sib", "col", None),
    )
    out_specs = P(("sib", "row", "col"), None)
    return jax.shard_map(body, mesh=mesh, in_specs=in_specs, out_specs=out_specs, check_vma=False)
```

```python
import functools

import jax
import jax.numpy as jnp
from jax import lax
from jax.experimental import pallas as pl
from jax.experimental.pallas import tpu as pltpu
from jax.sharding import PartitionSpec as P

LANES = 128
SUB = 64
PARTS = 1
STEPS = 32767.0
MESH = pl.DeviceIdType.MESH


def inverse(value):
    guess = pl.reciprocal(value, approx=True)
    return guess * (2.0 - value * guess)


def pick(tables, index):
    row, lane = index >> 7, index & (LANES - 1)
    picked = jnp.zeros(index.shape, jnp.float32)
    for t, table in enumerate(tables):
        there = jnp.take_along_axis(jnp.broadcast_to(table, index.shape), lane, axis=1)
        picked = jnp.where(row == t, there, picked)
    return picked


def kernel(n, eig, *refs):
    small_hbm, out, small = refs[:7], refs[7], refs[8:15]
    poles, weights, shifts, src, dst, cosines, sines = small
    (eig_buf, slab_own, slab_hi, slab_lo, shift_t, src_t, dst_t, cos_t, listed, inv,
     part_b, part_q, norm_acc, pair_send, pair_recv, norm_send, norm_recv,
     core_send, core_recv, chip_send, chip_recv, top_send, top_recv, both_acc,
     eig_sem, pair_ssem, pair_rsem, norm_ssem, norm_rsem,
     core_ssem, core_rsem, chip_ssem, chip_rsem, small_sem) = refs[15:]
    rows, width = eig_buf.shape
    block = rows // n
    piece = block // PARTS
    slab = shifts.shape[1]
    pairs = src.shape[2]
    tiles, lists = width // LANES, pairs // LANES
    chips = n // 2
    me = lax.axis_index("col")
    chip, core = me // 2, lax.rem(me, 2)
    other = 1 - core

    def col(index):
        return {"col": index}

    def peer(step):
        return lax.rem(me + step, n)

    small_loads = []
    for at, (source, target) in enumerate(zip(small_hbm, small)):
        load = pltpu.make_async_copy(source, target, small_sem.at[at])
        load.start()
        small_loads.append(load)

    barrier = pltpu.get_barrier_semaphore()
    for step in range(1, n):
        pl.semaphore_signal(barrier, inc=1, device_id=col(peer(step)), device_id_type=MESH)

    loads = []
    for part in range(4):
        span = pl.ds(part * (rows // 4), rows // 4)
        load = pltpu.make_async_copy(eig.at[0, span, :], eig_buf.at[span, :], eig_sem.at[part])
        load.start()
        loads.append(load)

    for load in small_loads:
        load.wait()

    listed[...] = jnp.zeros_like(listed)
    for r in range(lists):
        cut = slice(r * LANES, (r + 1) * LANES)
        listed[r:r + 1, :] = dst[0, :, cut]
    index = listed[...]
    pole_rows = [poles[:, t * LANES:(t + 1) * LANES] for t in range(tiles)]
    weight_rows = [weights[:, t * LANES:(t + 1) * LANES] for t in range(tiles)]
    pair_send[0] = pick(weight_rows, index)
    pair_send[1] = pick(pole_rows, index)
    for r in range(lists):
        cut = slice(r * LANES, (r + 1) * LANES)
        pair_send[0, r:r + 1, :] = pair_send[0, r:r + 1, :] * sines[0, :, cut]

    pl.semaphore_wait(barrier, n - 1)
    pair_copy = pltpu.make_async_remote_copy(
        src_ref=pair_send, dst_ref=pair_recv, send_sem=pair_ssem, recv_sem=pair_rsem,
        device_id=col(lax.rem(me + n // 2, n)), device_id_type=MESH)
    pair_copy.start()

    for r in range(lists):
        cut = slice(r * LANES, (r + 1) * LANES)
        src_t[cut, :] = jnp.broadcast_to(src[0, :, cut], (LANES, LANES)).T
        dst_t[cut, :] = jnp.broadcast_to(dst[0, :, cut], (LANES, LANES)).T
        cos_t[cut, :] = jnp.broadcast_to(cosines[0, :, cut], (LANES, LANES)).T - 1.0
    for r in range(slab // LANES):
        cut = slice(r * LANES, (r + 1) * LANES)
        shift_t[cut, :] = jnp.broadcast_to(shifts[:, cut], (LANES, LANES)).T
    norm_acc[...] = jnp.zeros_like(norm_acc)

    def own_part(t, carry):
        cut = pl.ds(pl.multiple_of(t * LANES, LANES), LANES)
        local = lax.broadcasted_iota(jnp.int32, (SUB, LANES), 1) + t * LANES
        turned = jnp.zeros((SUB, LANES), jnp.float32)
        place = jnp.zeros((SUB, LANES), jnp.int32)
        count = lax.broadcasted_iota(jnp.int32, (SUB, LANES), 0) + 1
        for r in range(0, pairs, SUB):
            turned = jnp.where(dst_t[r:r + SUB, :] == local, cos_t[r:r + SUB, :], turned)
            place = jnp.where(src_t[r:r + SUB, :] == local, count + r, place)
        cosfull = 1.0 + jnp.sum(turned, axis=0, keepdims=True)
        inv[pl.ds(t, 1), :] = jnp.sum(place, axis=0, keepdims=True)
        pole = poles[:, cut]
        weight = weights[:, cut]
        for r in range(0, slab, SUB):
            cauchy = weight * inverse(pole - shift_t[r:r + SUB, :])
            norm_acc[r:r + SUB, :] += cauchy * cauchy
            slab_own[r:r + SUB, cut] = cosfull * cauchy
        return carry

    lax.fori_loop(0, tiles, own_part, 0)

    norm_send[...] = jnp.broadcast_to(jnp.sum(norm_acc[...].T, axis=0, keepdims=True), norm_send.shape)
    norm_copies = []
    for step in range(1, n):
        copy = pltpu.make_async_remote_copy(
            src_ref=norm_send, dst_ref=norm_recv.at[step], send_sem=norm_ssem.at[step],
            recv_sem=norm_rsem.at[step], device_id=col(peer(step)), device_id_type=MESH)
        copy.start()
        norm_copies.append(copy)

    pair_copy.wait()
    for t in range(0, tiles, 8):
        place = inv[t:t + 8, :]
        at = jnp.maximum(place - 1, 0)
        part_b[t:t + 8, :] = jnp.where(place > 0, pick([pair_recv[0, r:r + 1, :] for r in range(lists)], at), 0.0)
        part_q[t:t + 8, :] = jnp.where(place > 0, pick([pair_recv[1, r:r + 1, :] for r in range(lists)], at), -1.0)

    def partner_part(t, carry):
        cut = pl.ds(pl.multiple_of(t * LANES, LANES), LANES)
        pole = part_q[pl.ds(t, 1), :]
        weight = part_b[pl.ds(t, 1), :]
        for r in range(0, slab, SUB):
            total = slab_own[r:r + SUB, cut] + weight * inverse(pole - shift_t[r:r + SUB, :])
            high = total.astype(jnp.bfloat16)
            slab_hi[r:r + SUB, cut] = high
            slab_lo[r:r + SUB, cut] = (total - high.astype(jnp.float32)).astype(jnp.bfloat16)
        return carry

    lax.fori_loop(0, tiles, partner_part, 0)

    for load in loads:
        load.wait()

    def product(owner_chip):
        first = pl.multiple_of(owner_chip * 2 * block, 2 * block)
        left = eig_buf[pl.ds(first, 2 * block), :]
        dims = (((1,), (1,)), ((), ()))
        return (lax.dot_general(left, slab_hi[...], dims, preferred_element_type=jnp.float32)
                + lax.dot_general(left, slab_lo[...], dims, preferred_element_type=jnp.float32))

    core_copies, chip_copies = {}, {}

    def to_core(step, part):
        copy = pltpu.make_async_remote_copy(
            src_ref=core_send.at[step, part], dst_ref=core_recv.at[step, part],
            send_sem=core_ssem.at[step, part], recv_sem=core_rsem.at[step, part],
            device_id=col(chip * 2 + other), device_id_type=MESH)
        copy.start()
        core_copies[step, part] = copy

    def to_chip(step, part, away):
        copies = []
        for at, (source, target) in enumerate(((chip_send, chip_recv), (top_send, top_recv))):
            copy = pltpu.make_async_remote_copy(
                src_ref=source.at[step, part], dst_ref=target.at[step, part],
                send_sem=chip_ssem.at[at, step, part], recv_sem=chip_rsem.at[at, step, part],
                device_id=col(away * 2 + core), device_id_type=MESH)
            copy.start()
            copies.append(copy)
        chip_copies[step, part] = copies

    for step in range(1, chips):
        away = lax.rem(chip + step, chips)
        both_acc[...] = product(away).reshape(both_acc.shape)
        core_send[step] = both_acc[other]
        for part in range(PARTS):
            to_core(step, part)
        for part in range(PARTS):
            core_copies[step, part].wait_recv()
            mine = both_acc[core, part] + core_recv[step, part]
            top = jnp.maximum(jnp.max(jnp.abs(mine), axis=0, keepdims=True), 1e-33)
            chip_send[step, part] = jnp.round(mine * (STEPS / top)).astype(jnp.int32).astype(jnp.int16)
            top_send[step, part] = jnp.broadcast_to(top, top_send.shape[2:])
            to_chip(step, part, away)
    both_acc[...] = product(chip).reshape(both_acc.shape)
    core_send[0] = both_acc[other]
    for part in range(PARTS):
        to_core(0, part)

    normsq = norm_send[0:1, :]
    for step, copy in enumerate(norm_copies):
        copy.wait()
        normsq = normsq + norm_recv[step + 1, 0:1, :]
    scale = jnp.sqrt(normsq)
    for part in range(PARTS):
        core_copies[0, part].wait_recv()
        total = both_acc[core, part] + core_recv[0, part]
        for step in range(1, chips):
            for copy in chip_copies[step, part]:
                copy.wait()
            unit = top_recv[step, part, 0:1, :] * (1.0 / STEPS)
            total = total + chip_recv[step, part].astype(jnp.int32).astype(jnp.float32) * unit
        out[part * piece:(part + 1) * piece, :] = (total / scale).astype(out.dtype)
    for copy in core_copies.values():
        copy.wait_send()


def body(eigvec, *small):
    n = lax.axis_size("col")
    _, rows, width = eigvec.shape
    slab = small[2].shape[1]
    pairs = small[3].shape[2]
    block = rows // n
    piece = block // PARTS
    chips = n // 2
    tiles = width // LANES
    f32, bf16 = jnp.float32, jnp.bfloat16
    vmem = pl.BlockSpec(memory_space=pltpu.VMEM)
    dma = pltpu.SemaphoreType.DMA
    return pl.pallas_call(
        functools.partial(kernel, n),
        out_shape=pltpu.VMEM((block, slab), bf16),
        in_specs=[pl.BlockSpec(memory_space=pltpu.HBM)] * 8,
        out_specs=vmem,
        scratch_shapes=[
            *(pltpu.VMEM(value.shape, value.dtype) for value in small),
            pltpu.VMEM((rows, width), bf16),
            pltpu.VMEM((slab, width), f32),
            pltpu.VMEM((slab, width), bf16),
            pltpu.VMEM((slab, width), bf16),
            pltpu.VMEM((slab, LANES), f32),
            pltpu.VMEM((pairs, LANES), jnp.int32),
            pltpu.VMEM((pairs, LANES), jnp.int32),
            pltpu.VMEM((pairs, LANES), f32),
            pltpu.VMEM((8, LANES), jnp.int32),
            pltpu.VMEM((tiles, LANES), jnp.int32),
            pltpu.VMEM((tiles, LANES), f32),
            pltpu.VMEM((tiles, LANES), f32),
            pltpu.VMEM((slab, LANES), f32),
            pltpu.VMEM((2, 8, LANES), f32),
            pltpu.VMEM((2, 8, LANES), f32),
            pltpu.VMEM((8, slab), f32),
            pltpu.VMEM((n, 8, slab), f32),
            pltpu.VMEM((chips, PARTS, piece, slab), f32),
            pltpu.VMEM((chips, PARTS, piece, slab), f32),
            pltpu.VMEM((chips, PARTS, piece, slab), jnp.int16),
            pltpu.VMEM((chips, PARTS, piece, slab), jnp.int16),
            pltpu.VMEM((chips, PARTS, 8, slab), f32),
            pltpu.VMEM((chips, PARTS, 8, slab), f32),
            pltpu.VMEM((2, PARTS, piece, slab), f32),
            dma((4,)), dma, dma, dma((n,)), dma((n,)),
            dma((chips, PARTS)), dma((chips, PARTS)), dma((2, chips, PARTS)), dma((2, chips, PARTS)), dma((7,)),
        ],
        compiler_params=pltpu.CompilerParams(
            collective_id=0, has_side_effects=True, vmem_limit_bytes=60 * 2**20),
        cost_estimate=pl.CostEstimate(
            flops=4 * rows * width * slab, bytes_accessed=2 * rows * width, transcendentals=2 * width * slab),
        name="merge",
    )(eigvec, *small)


def solution(mesh):
    in_specs = (
        P("sib", "row", "col"),
        P("sib", "col"),
        P("sib", "col"),
        P("sib", None),
        P("sib", "col", None),
        P("sib", "col", None),
        P("sib", "col", None),
        P("sib", "col", None),
    )
    out_specs = P(("sib", "row", "col"), None)
    return jax.shard_map(body, mesh=mesh, in_specs=in_specs, out_specs=out_specs, check_vma=False)
```

```python
import functools

import jax
import jax.numpy as jnp
from jax import lax
from jax.experimental import pallas as pl
from jax.experimental.pallas import tpu as pltpu
from jax.sharding import PartitionSpec as P

LANES = 128
SUB = 64
PARTS = 1
STEPS = 32767.0
MESH = pl.DeviceIdType.MESH


def inverse(value):
    guess = pl.reciprocal(value, approx=True)
    return guess * (2.0 - value * guess)


def pick(tables, index):
    row, lane = index >> 7, index & (LANES - 1)
    picked = jnp.zeros(index.shape, jnp.float32)
    for t, table in enumerate(tables):
        there = jnp.take_along_axis(jnp.broadcast_to(table, index.shape), lane, axis=1)
        picked = jnp.where(row == t, there, picked)
    return picked


def kernel(n, eig, *refs):
    small_hbm, out, small = refs[:7], refs[7], refs[8:15]
    poles, weights, shifts, src, dst, cosines, sines = small
    (eig_buf, slab_own, slab_hi, slab_lo, shift_t, src_t, dst_t, cos_t, listed, inv,
     part_b, part_q, norm_acc, pair_send, pair_recv, norm_send, norm_recv,
     core_send, core_recv, chip_send, chip_recv, top_send, top_recv, both_acc,
     eig_sem, pair_ssem, pair_rsem, norm_ssem, norm_rsem,
     core_ssem, core_rsem, chip_ssem, chip_rsem, small_sem) = refs[15:]
    rows, width = eig_buf.shape
    block = rows // n
    piece = block // PARTS
    slab = shifts.shape[1]
    pairs = src.shape[2]
    tiles, lists = width // LANES, pairs // LANES
    chips = n // 2
    me = lax.axis_index("col")
    chip, core = me // 2, lax.rem(me, 2)
    other = 1 - core

    def col(index):
        return {"col": index}

    def peer(step):
        return lax.rem(me + step, n)

    small_loads = []
    for at, (source, target) in enumerate(zip(small_hbm, small)):
        load = pltpu.make_async_copy(source, target, small_sem.at[at])
        load.start()
        small_loads.append(load)

    barrier = pltpu.get_barrier_semaphore()
    for step in range(1, n):
        pl.semaphore_signal(barrier, inc=1, device_id=col(peer(step)), device_id_type=MESH)

    loads = []
    for part in range(4):
        span = pl.ds(part * (rows // 4), rows // 4)
        load = pltpu.make_async_copy(eig.at[0, span, :], eig_buf.at[span, :], eig_sem.at[part])
        load.start()
        loads.append(load)

    for load in small_loads:
        load.wait()

    listed[...] = jnp.zeros_like(listed)
    for r in range(lists):
        cut = slice(r * LANES, (r + 1) * LANES)
        listed[r:r + 1, :] = dst[0, :, cut]
    index = listed[...]
    pole_rows = [poles[:, t * LANES:(t + 1) * LANES] for t in range(tiles)]
    weight_rows = [weights[:, t * LANES:(t + 1) * LANES] for t in range(tiles)]
    pair_send[0] = pick(weight_rows, index)
    pair_send[1] = pick(pole_rows, index)
    for r in range(lists):
        cut = slice(r * LANES, (r + 1) * LANES)
        pair_send[0, r:r + 1, :] = pair_send[0, r:r + 1, :] * sines[0, :, cut]

    pl.semaphore_wait(barrier, n - 1)
    pair_copy = pltpu.make_async_remote_copy(
        src_ref=pair_send, dst_ref=pair_recv, send_sem=pair_ssem, recv_sem=pair_rsem,
        device_id=col(lax.rem(me + n // 2, n)), device_id_type=MESH)
    pair_copy.start()

    for r in range(lists):
        cut = slice(r * LANES, (r + 1) * LANES)
        src_t[cut, :] = jnp.broadcast_to(src[0, :, cut], (LANES, LANES)).T
        dst_t[cut, :] = jnp.broadcast_to(dst[0, :, cut], (LANES, LANES)).T
        cos_t[cut, :] = jnp.broadcast_to(cosines[0, :, cut], (LANES, LANES)).T - 1.0
    for r in range(slab // LANES):
        cut = slice(r * LANES, (r + 1) * LANES)
        shift_t[cut, :] = jnp.broadcast_to(shifts[:, cut], (LANES, LANES)).T
    norm_acc[...] = jnp.zeros_like(norm_acc)

    def own_part(t, carry):
        cut = pl.ds(pl.multiple_of(t * LANES, LANES), LANES)
        local = lax.broadcasted_iota(jnp.int32, (SUB, LANES), 1) + t * LANES
        turned = jnp.zeros((SUB, LANES), jnp.float32)
        place = jnp.zeros((SUB, LANES), jnp.int32)
        count = lax.broadcasted_iota(jnp.int32, (SUB, LANES), 0) + 1
        for r in range(0, pairs, SUB):
            turned = jnp.where(dst_t[r:r + SUB, :] == local, cos_t[r:r + SUB, :], turned)
            place = jnp.where(src_t[r:r + SUB, :] == local, count + r, place)
        cosfull = 1.0 + jnp.sum(turned, axis=0, keepdims=True)
        inv[pl.ds(t, 1), :] = jnp.sum(place, axis=0, keepdims=True)
        pole = poles[:, cut]
        weight = weights[:, cut]
        for r in range(0, slab, SUB):
            cauchy = weight * inverse(pole - shift_t[r:r + SUB, :])
            norm_acc[r:r + SUB, :] += cauchy * cauchy
            slab_own[r:r + SUB, cut] = cosfull * cauchy
        return carry

    lax.fori_loop(0, tiles, own_part, 0)

    norm_send[...] = jnp.broadcast_to(jnp.sum(norm_acc[...].T, axis=0, keepdims=True), norm_send.shape)
    norm_copies = []
    for step in range(1, n):
        copy = pltpu.make_async_remote_copy(
            src_ref=norm_send, dst_ref=norm_recv.at[step], send_sem=norm_ssem.at[step],
            recv_sem=norm_rsem.at[step], device_id=col(peer(step)), device_id_type=MESH)
        copy.start()
        norm_copies.append(copy)

    pair_copy.wait()
    for t in range(0, tiles, 8):
        place = inv[t:t + 8, :]
        at = jnp.maximum(place - 1, 0)
        part_b[t:t + 8, :] = jnp.where(place > 0, pick([pair_recv[0, r:r + 1, :] for r in range(lists)], at), 0.0)
        part_q[t:t + 8, :] = jnp.where(place > 0, pick([pair_recv[1, r:r + 1, :] for r in range(lists)], at), -1.0)

    def partner_part(t, carry):
        cut = pl.ds(pl.multiple_of(t * LANES, LANES), LANES)
        pole = part_q[pl.ds(t, 1), :]
        weight = part_b[pl.ds(t, 1), :]
        for r in range(0, slab, SUB):
            total = slab_own[r:r + SUB, cut] + weight * inverse(pole - shift_t[r:r + SUB, :])
            high = total.astype(jnp.bfloat16)
            slab_hi[r:r + SUB, cut] = high
            slab_lo[r:r + SUB, cut] = (total - high.astype(jnp.float32)).astype(jnp.bfloat16)
        return carry

    lax.fori_loop(0, tiles, partner_part, 0, unroll=4)

    for load in loads:
        load.wait()

    def product(owner_chip):
        first = pl.multiple_of(owner_chip * 2 * block, 2 * block)
        left = eig_buf[pl.ds(first, 2 * block), :]
        dims = (((1,), (1,)), ((), ()))
        return (lax.dot_general(left, slab_hi[...], dims, preferred_element_type=jnp.float32)
                + lax.dot_general(left, slab_lo[...], dims, preferred_element_type=jnp.float32))

    core_copies, chip_copies = {}, {}

    def to_core(step, part):
        copy = pltpu.make_async_remote_copy(
            src_ref=core_send.at[step, part], dst_ref=core_recv.at[step, part],
            send_sem=core_ssem.at[step, part], recv_sem=core_rsem.at[step, part],
            device_id=col(chip * 2 + other), device_id_type=MESH)
        copy.start()
        core_copies[step, part] = copy

    def to_chip(step, part, away):
        copies = []
        for at, (source, target) in enumerate(((chip_send, chip_recv), (top_send, top_recv))):
            copy = pltpu.make_async_remote_copy(
                src_ref=source.at[step, part], dst_ref=target.at[step, part],
                send_sem=chip_ssem.at[at, step, part], recv_sem=chip_rsem.at[at, step, part],
                device_id=col(away * 2 + core), device_id_type=MESH)
            copy.start()
            copies.append(copy)
        chip_copies[step, part] = copies

    for step in range(1, chips):
        away = lax.rem(chip + step, chips)
        both_acc[...] = product(away).reshape(both_acc.shape)
        core_send[step] = both_acc[other]
        for part in range(PARTS):
            to_core(step, part)
        for part in range(PARTS):
            core_copies[step, part].wait_recv()
            mine = both_acc[core, part] + core_recv[step, part]
            top = jnp.maximum(jnp.max(jnp.abs(mine), axis=0, keepdims=True), 1e-33)
            chip_send[step, part] = jnp.round(mine * (STEPS / top)).astype(jnp.int32).astype(jnp.int16)
            top_send[step, part] = jnp.broadcast_to(top, top_send.shape[2:])
            to_chip(step, part, away)
    both_acc[...] = product(chip).reshape(both_acc.shape)
    core_send[0] = both_acc[other]
    for part in range(PARTS):
        to_core(0, part)

    normsq = norm_send[0:1, :]
    for step, copy in enumerate(norm_copies):
        copy.wait()
        normsq = normsq + norm_recv[step + 1, 0:1, :]
    scale = jnp.sqrt(normsq)
    for part in range(PARTS):
        core_copies[0, part].wait_recv()
        total = both_acc[core, part] + core_recv[0, part]
        for step in range(1, chips):
            for copy in chip_copies[step, part]:
                copy.wait()
            unit = top_recv[step, part, 0:1, :] * (1.0 / STEPS)
            total = total + chip_recv[step, part].astype(jnp.int32).astype(jnp.float32) * unit
        out[part * piece:(part + 1) * piece, :] = (total / scale).astype(out.dtype)
    for copy in core_copies.values():
        copy.wait_send()


def body(eigvec, *small):
    n = lax.axis_size("col")
    _, rows, width = eigvec.shape
    slab = small[2].shape[1]
    pairs = small[3].shape[2]
    block = rows // n
    piece = block // PARTS
    chips = n // 2
    tiles = width // LANES
    f32, bf16 = jnp.float32, jnp.bfloat16
    vmem = pl.BlockSpec(memory_space=pltpu.VMEM)
    dma = pltpu.SemaphoreType.DMA
    return pl.pallas_call(
        functools.partial(kernel, n),
        out_shape=pltpu.VMEM((block, slab), bf16),
        in_specs=[pl.BlockSpec(memory_space=pltpu.HBM)] * 8,
        out_specs=vmem,
        scratch_shapes=[
            *(pltpu.VMEM(value.shape, value.dtype) for value in small),
            pltpu.VMEM((rows, width), bf16),
            pltpu.VMEM((slab, width), f32),
            pltpu.VMEM((slab, width), bf16),
            pltpu.VMEM((slab, width), bf16),
            pltpu.VMEM((slab, LANES), f32),
            pltpu.VMEM((pairs, LANES), jnp.int32),
            pltpu.VMEM((pairs, LANES), jnp.int32),
            pltpu.VMEM((pairs, LANES), f32),
            pltpu.VMEM((8, LANES), jnp.int32),
            pltpu.VMEM((tiles, LANES), jnp.int32),
            pltpu.VMEM((tiles, LANES), f32),
            pltpu.VMEM((tiles, LANES), f32),
            pltpu.VMEM((slab, LANES), f32),
            pltpu.VMEM((2, 8, LANES), f32),
            pltpu.VMEM((2, 8, LANES), f32),
            pltpu.VMEM((8, slab), f32),
            pltpu.VMEM((n, 8, slab), f32),
            pltpu.VMEM((chips, PARTS, piece, slab), f32),
            pltpu.VMEM((chips, PARTS, piece, slab), f32),
            pltpu.VMEM((chips, PARTS, piece, slab), jnp.int16),
            pltpu.VMEM((chips, PARTS, piece, slab), jnp.int16),
            pltpu.VMEM((chips, PARTS, 8, slab), f32),
            pltpu.VMEM((chips, PARTS, 8, slab), f32),
            pltpu.VMEM((2, PARTS, piece, slab), f32),
            dma((4,)), dma, dma, dma((n,)), dma((n,)),
            dma((chips, PARTS)), dma((chips, PARTS)), dma((2, chips, PARTS)), dma((2, chips, PARTS)), dma((7,)),
        ],
        compiler_params=pltpu.CompilerParams(
            collective_id=0, has_side_effects=True, vmem_limit_bytes=60 * 2**20),
        cost_estimate=pl.CostEstimate(
            flops=4 * rows * width * slab, bytes_accessed=2 * rows * width, transcendentals=2 * width * slab),
        name="merge",
    )(eigvec, *small)


def solution(mesh):
    in_specs = (
        P("sib", "row", "col"),
        P("sib", "col"),
        P("sib", "col"),
        P("sib", None),
        P("sib", "col", None),
        P("sib", "col", None),
        P("sib", "col", None),
        P("sib", "col", None),
    )
    out_specs = P(("sib", "row", "col"), None)
    return jax.shard_map(body, mesh=mesh, in_specs=in_specs, out_specs=out_specs, check_vma=False)
```
